32 devices in a mesh: dp: 4 (over y, x), ctx: 8 (over z, core).
Axes of the slice: x: 2, y: 2, z: 4, core: 2. Of those that a mesh axis runs over, the one named last changes fastest.
Arguments:
- resid: bfloat16 [4096, 2048], P(('dp', 'ctx')), may hold values from -6 to 6
- queries: bfloat16 [4096, 2048], P(('dp', 'ctx')), may hold values from -28 to 28
- keys: bfloat16 [4096, 128], P(('dp', 'ctx')), may hold values from -6 to 6
- values: bfloat16 [4096, 128], P(('dp', 'ctx')), may hold values from -6 to 6
- block_order: int32 [16], replicated, may hold values from 0 to 15, each once
- routes: int32 [4096, 4], P(('dp', 'ctx')), may hold values from 0 to 31, all different within a row; in each aligned block of 128 rows (0 to 127, 128 to 255, ...) at most 20 rows name the same one
- route_weights: float32 [4096, 4], P(('dp', 'ctx')), may hold values from 0.1 to 1
- norm_gain: float32 [2048], replicated, may hold values from 0.5 to 2
- w_gate: bfloat16 [32, 2048, 768], P(('dp', 'ctx')), may hold values from -0.125 to 0.125
- w_up: bfloat16 [32, 2048, 768], P(('dp', 'ctx')), may hold values from -0.125 to 0.125
- w_down: bfloat16 [32, 768, 2048], P(('dp', 'ctx')), may hold values from -0.21875 to 0.21875
- cotangent: bfloat16 [4096, 2048], P(('dp', 'ctx')), may hold values from -6 to 6
Outputs:
- layer_out: bfloat16 [4096, 2048], P(('dp', 'ctx'))
- d_resid: bfloat16 [4096, 2048], P(('dp', 'ctx'))
- d_queries: bfloat16 [4096, 2048], P(('dp', 'ctx'))
- d_keys: bfloat16 [4096, 128], P(('dp', 'ctx'))
- d_values: bfloat16 [4096, 128], P(('dp', 'ctx'))
- d_gain: float32 [2048], replicated
- d_w_gate: bfloat16 [32, 2048, 768], P(('dp', 'ctx'))
- d_w_up: bfloat16 [32, 2048, 768], P(('dp', 'ctx'))
- d_w_down: bfloat16 [32, 768, 2048], P(('dp', 'ctx'))
The draws below stay inside these ranges and needn't reach their ends.
Inputs may be any that keep to these rules, and one draw needn't show every extreme that they name: `routes`: each row names 4 different experts; the rows of one device name one expert at most 20 times, and that many in some device of every draw. `block_order`: each block number once.
All inputs are finite; a program needn't handle non-finite values.
Results may differ from the reference program's by a relative error of at most 0.023.
Values may be sent and summed in bfloat16 or wider, within the bound.
A program may use at most 128 MiB of HBM per device.

```python
import math
import jax
import jax.numpy as jnp
import numpy as np
from jax import lax

D = 2048
HQ = 32
HK = 2
DH = 64
FF = 768
TOP = 4
TOK_DEV = 128
BLOCK = 64
BLOCKS = 16
SEQ_LEN = 1024
TOKENS = 4096
EXPERTS = 32
CAP = 20
N_DP = 4


def draw_queries(key, part):
    key = jax.random.fold_in(key, 1)
    base = jnp.clip(jax.random.normal(key, (TOKENS, HQ * DH), jnp.float32), -6.0, 6.0)
    return base.astype(jnp.bfloat16)


def draw_keys(key, part):
    key = jax.random.fold_in(key, 2)
    base = jnp.clip(jax.random.normal(key, (TOKENS, HK * DH), jnp.float32), -6.0, 6.0)
    return base.astype(jnp.bfloat16)


def level_of(stream_key, shape, shards, low, top_value):
    loudness, own = 1.0, jax.random.fold_in(stream_key, 6)
    for axis_at, parts in shards:
        draws = jnp.exp(jax.random.uniform(jax.random.fold_in(own, axis_at), (parts,), jnp.float32, low / len(shards), top_value / len(shards)))
        loudness = loudness * jnp.repeat(draws, shape[axis_at] // parts).reshape([-1 if axis == axis_at else 1 for axis in range(len(shape))])
    return loudness


def shared_out(key, own, number, rows, count, top, bound, lean):
    sequence = jax.random.permutation(key, count)
    heavy_load, ordinary = portions_of(count, rows * top, bound, lean, True), portions_of(count, rows * top, bound, lean, False)
    places = jnp.arange(count)

    def named(sizes, offset_by):
        used = int((sizes > 0).sum())
        fixed = max(1, used // 4)
        moved = fixed + (places - fixed + offset_by * (used - fixed)) % max(1, count - fixed)
        return jnp.zeros((count,), jnp.int32).at[sequence[jnp.where(places < fixed, places, moved)]].set(jnp.asarray(sizes, jnp.int32))

    sizes = jnp.where(number % 4 == 0, named(heavy_load, number // 4), named(ordinary, number - number // 4 - 1))
    mixed = jax.random.permutation(jax.random.fold_in(own, 3), count)
    source_of, receiver = mixed[0:count // 2 * 2:2], mixed[1:count // 2 * 2:2]
    margin = jnp.minimum(sizes[source_of] - 1, bound - sizes[receiver]) // 2
    margin = jnp.where((source_of == sequence[0]) | (receiver == sequence[0]) | (sizes[receiver] == 0), 0, jnp.maximum(margin, 0))
    moved = jax.random.randint(jax.random.fold_in(own, 4), (count // 2,), 0, 1 << 20) % (margin + 1)
    sizes = sizes.at[source_of].add(-moved).at[receiver].add(moved)
    items = jnp.searchsorted(jnp.cumsum(sizes), jnp.arange(rows * top), side="right").astype(jnp.int32)
    grid = items.reshape(top, rows).T
    grid = grid[jax.random.permutation(jax.random.fold_in(own, 1), rows)]
    offset_by = jax.random.randint(jax.random.fold_in(own, 2), (rows, 1), 0, top)
    return jnp.take_along_axis(grid, (jnp.arange(top)[None, :] + offset_by) % top, axis=1)


def portions_of(count, total, most, slope, full):
    portions = [(1 << 20) // math.isqrt(standing ** slope) + 1 for standing in range(1, count + 1)]
    largest = most if full else min(most, max(-(-total // count), total * portions[0] // sum(portions)))
    least = 1 if total - largest >= count - 1 else 0
    holding, rest = [largest] + [least] * (count - 1), total - largest - least * (count - 1)
    while rest > 0:
        movable = [i for i in range(1, count) if holding[i] < largest] or [i for i in range(1, count) if holding[i] < most]
        mass, budget = sum([portions[i] for i in movable]), rest
        for i in movable:
            extra = min(most - holding[i], max(1, budget * portions[i] // mass), rest)
            holding[i] = holding[i] + extra
            rest = rest - extra
    return np.array(holding)


def normal_values(stream_key, dims, deviation, reach, cuts=(), kind=jnp.bfloat16):
    drawn = jax.random.normal(stream_key, dims, jnp.float32) * deviation
    if len(cuts) > 0:
        drawn = level_of(stream_key, dims, cuts, -0.22, 0.18) * drawn
    return jnp.clip(drawn, min=-reach, max=reach).astype(kind)


def setup_inputs(seed: int = 0) -> dict:
    key_of = jax.random.split(jax.random.key(seed), 13)
    resid = normal_values(key_of[0], (TOKENS, D), 1.0, 6.0, ((0, 32),))
    queries = draw_queries(jax.random.fold_in(key_of[12], 71), 0)
    keys = draw_keys(jax.random.fold_in(key_of[12], 71), 0)
    values = normal_values(key_of[3], (TOKENS, HK * DH), 1.0, 6.0, ((0, 32),))
    block_order = jax.random.permutation(key_of[4], BLOCKS).astype(jnp.int32)
    routes_keys = jax.random.split(jax.random.fold_in(key_of[5], 1), TOKENS // TOK_DEV)
    routes_turns = jax.random.permutation(jax.random.fold_in(key_of[5], 3), TOKENS // TOK_DEV)
    routes = jax.vmap(lambda own, number: shared_out(jax.random.fold_in(key_of[5], 2), own, number, TOK_DEV, EXPERTS, TOP, CAP, 1))(routes_keys, routes_turns).reshape((TOKENS, TOP))
    route_weights = jnp.clip(0.1 + 0.9 * jax.random.uniform(key_of[6], (TOKENS, TOP), jnp.float32) ** level_of(key_of[6], (TOKENS, TOP), ((0, 32),), -0.2, 0.2), 0.1, 1.0)
    norm_gain = jnp.clip(jax.random.uniform(key_of[7], (D,), jnp.float32, 0.5, 2.0), 0.5, 2.0)
    w_gate = normal_values(key_of[8], (EXPERTS, D, FF), D ** -0.5, 0.125, ((0, 32),))
    w_up = normal_values(key_of[9], (EXPERTS, D, FF), D ** -0.5, 0.125, ((0, 32),))
    w_down = normal_values(key_of[10], (EXPERTS, FF, D), FF ** -0.5, 0.21875, ((0, 32),))
    cotangent = normal_values(key_of[11], (TOKENS, D), 1.0, 6.0, ((0, 32),))
    return {"resid": resid, "queries": queries, "keys": keys, "values": values, "block_order": block_order, "routes": routes, "route_weights": route_weights, "norm_gain": norm_gain, "w_gate": w_gate, "w_up": w_up, "w_down": w_down, "cotangent": cotangent}


NEG_BIG = -1e+30
EPSILON = 1e-06

def round_half(values):
    return lax.optimization_barrier(values.astype(jnp.bfloat16)).astype(jnp.float32)

def sequence_places(block_order):
    rows_seq = jnp.arange(SEQ_LEN, dtype=jnp.int32)
    return (block_order[rows_seq // BLOCK] * BLOCK + rows_seq % BLOCK).astype(jnp.int32)

def head_views(query_rows, key_rows, value_rows):
    query_heads = query_rows.astype(jnp.float32).reshape(SEQ_LEN, HK, HQ // HK, DH)
    key_heads = key_rows.astype(jnp.float32).reshape(SEQ_LEN, HK, DH)
    value_heads = value_rows.astype(jnp.float32).reshape(SEQ_LEN, HK, DH)
    return (query_heads, key_heads, value_heads)

def masked_scores(query_heads, key_heads, places):
    scores = jnp.einsum('tkgd,pkd->kgtp', query_heads, key_heads) * DH ** (-0.5)
    allowed = places[:, None] >= places[None, :]
    return jnp.where(allowed, scores, NEG_BIG)

def attend_forward(places, operands):
    query_heads, key_heads, value_heads = head_views(operands[0], operands[1], operands[2])
    scores = masked_scores(query_heads, key_heads, places)
    row_top = lax.optimization_barrier(jnp.max(scores, axis=-1))
    weights = jnp.exp(scores - row_top[..., None])
    totals = lax.optimization_barrier(jnp.sum(weights, axis=-1))
    mixed = jnp.einsum('kgtp,pkd->tkgd', round_half(weights), value_heads)
    mixed = mixed / jnp.transpose(totals, (2, 0, 1))[..., None]
    return (mixed.reshape(SEQ_LEN, HQ * DH).astype(jnp.bfloat16), row_top + jnp.log(totals))

def attend_backward(places, operands):
    query_heads, key_heads, value_heads = head_views(operands[0], operands[1], operands[2])
    attended, log_totals, grad_rows = (operands[3], operands[4], operands[5])
    scores = masked_scores(query_heads, key_heads, places)
    probabilities = jnp.exp(scores - log_totals[..., None])
    grad_heads = grad_rows.astype(jnp.float32).reshape(SEQ_LEN, HK, HQ // HK, DH)
    out_heads = attended.astype(jnp.float32).reshape(SEQ_LEN, HK, HQ // HK, DH)
    row_dots = jnp.transpose(lax.optimization_barrier(jnp.sum(grad_heads * out_heads, axis=-1)), (1, 2, 0))
    grad_values = jnp.einsum('kgtp,tkgd->pkd', round_half(probabilities), grad_heads)
    grad_probs = jnp.einsum('tkgd,pkd->kgtp', grad_heads, value_heads)
    grad_scores = round_half(probabilities * (grad_probs - row_dots[..., None]) * DH ** (-0.5))
    grad_queries = jnp.einsum('kgtp,pkd->tkgd', grad_scores, key_heads)
    grad_keys = jnp.einsum('kgtp,tkgd->pkd', grad_scores, query_heads)
    return (grad_queries.reshape(SEQ_LEN, HQ * DH).astype(jnp.bfloat16), grad_keys.reshape(SEQ_LEN, HK * DH).astype(jnp.bfloat16), grad_values.reshape(SEQ_LEN, HK * DH).astype(jnp.bfloat16))

def expert_block(operands):
    rows_in, grads_in, gate_w, up_w, down_w = operands
    rows_flat = rows_in.reshape(-1, D)
    grads_flat = grads_in.reshape(-1, D)
    gate_lin = jnp.dot(rows_flat, gate_w, preferred_element_type=jnp.float32)
    up_lin = jnp.dot(rows_flat, up_w, preferred_element_type=jnp.float32)
    gate_sig = jax.nn.sigmoid(gate_lin)
    gate_act = gate_lin * gate_sig
    hidden_act = (gate_act * up_lin).astype(jnp.bfloat16)
    produced = jnp.dot(hidden_act, down_w, preferred_element_type=jnp.float32).astype(jnp.bfloat16)
    grad_act = jnp.dot(grads_flat, down_w.T, preferred_element_type=jnp.float32)
    grad_gate = (grad_act * up_lin * gate_sig * (1.0 + gate_lin * (1.0 - gate_sig))).astype(jnp.bfloat16)
    grad_up = (grad_act * gate_act).astype(jnp.bfloat16)
    grad_in = (jnp.dot(grad_gate, gate_w.T, preferred_element_type=jnp.float32) + jnp.dot(grad_up, up_w.T, preferred_element_type=jnp.float32)).astype(jnp.bfloat16)
    grad_gate_w = jnp.dot(rows_flat.T, grad_gate, preferred_element_type=jnp.float32).astype(jnp.bfloat16)
    grad_up_w = jnp.dot(rows_flat.T, grad_up, preferred_element_type=jnp.float32).astype(jnp.bfloat16)
    grad_down_w = jnp.dot(hidden_act.T, grads_flat, preferred_element_type=jnp.float32).astype(jnp.bfloat16)
    return (produced.reshape(rows_in.shape), grad_in.reshape(rows_in.shape), grad_gate_w, grad_up_w, grad_down_w)

def reference(resid, queries, keys, values, block_order, routes, route_weights, norm_gain, w_gate, w_up, w_down, cotangent):
    places = sequence_places(block_order)
    query_seq = queries.reshape(N_DP, SEQ_LEN, HQ * DH)
    key_seq = keys.reshape(N_DP, SEQ_LEN, HK * DH)
    value_seq = values.reshape(N_DP, SEQ_LEN, HK * DH)
    attended, log_totals = lax.map(lambda operands: attend_forward(places, operands), (query_seq, key_seq, value_seq))
    attended_rows = attended.reshape(TOKENS, HQ * DH)
    hidden = (resid.astype(jnp.float32) + attended_rows.astype(jnp.float32)).astype(jnp.bfloat16)
    hidden_f = hidden.astype(jnp.float32)
    inv_rms = lax.rsqrt(lax.optimization_barrier(jnp.mean(hidden_f * hidden_f, axis=-1, keepdims=True)) + EPSILON)
    normed = (hidden_f * inv_rms * norm_gain).astype(jnp.bfloat16)
    blocks = TOKENS // TOK_DEV
    flat_routes = routes.reshape(blocks, TOK_DEV * TOP)
    onehot = (flat_routes[..., None] == jnp.arange(EXPERTS, dtype=jnp.int32)).astype(jnp.int32)
    slot_rank = (lax.optimization_barrier(jnp.sum(jnp.cumsum(onehot, axis=1) * onehot, axis=-1)) - 1).reshape(TOKENS, TOP).astype(jnp.int32)
    owners = jnp.broadcast_to((jnp.arange(TOKENS, dtype=jnp.int32) // TOK_DEV)[:, None], (TOKENS, TOP))
    empty_rows = jnp.zeros((EXPERTS, blocks, CAP, D), jnp.bfloat16)
    send_rows = empty_rows.at[routes, owners, slot_rank].set(jnp.broadcast_to(normed[:, None, :], (TOKENS, TOP, D)))
    grad_out = cotangent.astype(jnp.float32)
    grad_slot = (route_weights[..., None] * grad_out[:, None, :]).astype(jnp.bfloat16)
    grad_rows = empty_rows.at[routes, owners, slot_rank].set(grad_slot)
    produced, grad_in, d_w_gate, d_w_up, d_w_down = lax.map(expert_block, (send_rows, grad_rows, w_gate, w_up, w_down))
    returned = produced[routes, owners, slot_rank].astype(jnp.float32)
    mixed_moe = lax.optimization_barrier(jnp.sum(route_weights[..., None] * returned, axis=1))
    layer_out = (hidden_f + mixed_moe).astype(jnp.bfloat16)
    grad_normed = lax.optimization_barrier(jnp.sum(grad_in[routes, owners, slot_rank].astype(jnp.float32), axis=1))
    grad_scaled = grad_normed * norm_gain
    grad_hidden = inv_rms * grad_scaled - hidden_f * inv_rms * inv_rms * inv_rms * lax.optimization_barrier(jnp.mean(grad_scaled * hidden_f, axis=-1, keepdims=True))
    d_gain = lax.optimization_barrier(jnp.sum(grad_normed * hidden_f * inv_rms, axis=0))
    d_resid = (grad_out + grad_hidden).astype(jnp.bfloat16)
    backward_in = (query_seq, key_seq, value_seq, attended, log_totals, d_resid.reshape(N_DP, SEQ_LEN, D))
    d_queries, d_keys, d_values = lax.map(lambda operands: attend_backward(places, operands), backward_in)
    return (layer_out, d_resid, d_queries.reshape(TOKENS, HQ * DH), d_keys.reshape(TOKENS, HK * DH), d_values.reshape(TOKENS, HK * DH), d_gain, d_w_gate, d_w_up, d_w_down)
```

```python
import functools

import jax
import jax.numpy as jnp
from jax import lax
from jax.experimental import pallas as pl
from jax.experimental.pallas import tpu as pltpu
from jax.sharding import PartitionSpec as P

DH = 64
NEG_BIG = -1e30
EPSILON = 1e-06
F32 = jnp.float32
BF16 = jnp.bfloat16
VMEM_BYTES = 48 * 1024 * 1024


def dot_nn(a, b):
    return lax.dot_general(a, b, (((1,), (0,)), ((), ())), preferred_element_type=F32)


def dot_nt(a, b):
    return lax.dot_general(a, b, (((1,), (1,)), ((), ())), preferred_element_type=F32)


def dot_tn(a, b):
    return lax.dot_general(a, b, (((0,), (0,)), ((), ())), preferred_element_type=F32)


def twin(block, head):
    lane = lax.broadcasted_iota(jnp.int32, block.shape, 1)
    turned = jnp.concatenate([block[:, DH:], block[:, :DH]], axis=1)
    return jnp.where((lane < DH) == (head == 0), block, turned)


def spread(block):
    lane = lax.broadcasted_iota(jnp.int32, block.shape, 1)
    zero = jnp.zeros_like(block)
    return jnp.concatenate(
        [jnp.where(lane < DH, block, zero), jnp.where(lane >= DH, block, zero)], axis=0
    )


def unspread(stacked):
    rows = stacked.shape[0] // 2
    lane = lax.broadcasted_iota(jnp.int32, (rows, stacked.shape[1]), 1)
    return jnp.where(lane < DH, stacked[:rows], stacked[rows:])


def prepare(kv_ref, qplace_ref, kplace_ref, bias, twins):
    width = kv_ref.shape[1] // 2
    bias[...] = jnp.where(qplace_ref[...] >= kplace_ref[...], 0.0, NEG_BIG).astype(F32)
    for part in range(2):
        block = kv_ref[:, part * width : (part + 1) * width].astype(F32)
        for head in range(2):
            twins[part, head] = twin(block, head).astype(BF16)


def masked_scores(q2, keys2, bias):
    scores = dot_nt(q2, keys2) * (DH**-0.5)
    rows = bias.shape[0]
    return jnp.concatenate([scores[:rows] + bias[...], scores[rows:] + bias[...]], axis=0)


def forward_kernel(pairs, q_ref, kv_ref, qplace_ref, kplace_ref, out_ref, lse_ref, bias, twins):
    step = pl.program_id(0)

    @pl.when(step == 0)
    def _():
        prepare(kv_ref, qplace_ref, kplace_ref, bias, twins)

    group = step // (pairs // 2)
    scores = masked_scores(spread(q_ref[...]), twins[0, group], bias)
    top = jnp.max(scores, axis=1, keepdims=True)
    weights = jnp.exp(scores - top)
    total = jnp.sum(weights, axis=1, keepdims=True)
    mixed = dot_nn(weights.astype(BF16), twins[1, group])
    out_ref[...] = unspread(mixed / total).astype(BF16)
    lse_ref[0] = top + jnp.log(total)


def backward_kernel(
    pairs,
    q_ref,
    kv_ref,
    qplace_ref,
    kplace_ref,
    att_ref,
    lse_ref,
    grad_ref,
    dq_ref,
    dkv_ref,
    bias,
    twins,
    sums,
):
    step = pl.program_id(0)

    @pl.when(step == 0)
    def _():
        prepare(kv_ref, qplace_ref, kplace_ref, bias, twins)
        sums[...] = jnp.zeros_like(sums)

    group = step // (pairs // 2)
    q2 = spread(q_ref[...])
    g2 = spread(grad_ref[...])
    keys2 = twins[0, group]
    probs = jnp.exp(masked_scores(q2, keys2, bias) - lse_ref[0])
    product = grad_ref[...].astype(F32) * att_ref[...].astype(F32)
    row_dots = jnp.sum(spread(product), axis=1, keepdims=True)
    grad_probs = dot_nt(g2, twins[1, group])
    grad_scores = (probs * (grad_probs - row_dots) * (DH**-0.5)).astype(BF16)
    dq_ref[...] = unspread(dot_nn(grad_scores, keys2)).astype(BF16)
    sums[0, group] += dot_tn(grad_scores, q2)
    sums[1, group] += dot_tn(probs.astype(BF16), g2)

    @pl.when(step == pairs - 1)
    def _():
        width = dkv_ref.shape[1] // 2
        for part in range(2):
            folded = []
            for head in range(2):
                both = sums[part, head]
                folded.append(
                    both + jnp.concatenate([both[:, DH:], both[:, :DH]], axis=1)
                )
            lane = lax.broadcasted_iota(jnp.int32, folded[0].shape, 1)
            dkv_ref[:, part * width : (part + 1) * width] = jnp.where(
                lane < DH, folded[0], folded[1]
            ).astype(BF16)


def attention_specs(rows, seq):
    pair = pl.BlockSpec((rows, 2 * DH), lambda i: (0, i))
    lse = pl.BlockSpec((1, 2 * rows, 1), lambda i: (i, 0, 0))
    full = lambda shape: pl.BlockSpec(shape, lambda i: (0, 0))
    common = [pair, full((seq, 4 * DH)), full((rows, 1)), full((1, seq))]
    scratch = [pltpu.VMEM((rows, seq), F32), pltpu.VMEM((2, 2, seq, 2 * DH), BF16)]
    return pair, lse, full, common, scratch


def attend_forward(queries, kv, qplace, kplace):
    rows, width = queries.shape
    seq = kv.shape[0]
    pairs = width // (2 * DH)
    pair, lse, full, common, scratch = attention_specs(rows, seq)
    return pl.pallas_call(
        functools.partial(forward_kernel, pairs),
        grid=(pairs,),
        in_specs=common,
        out_specs=[pair, lse],
        out_shape=[
            jax.ShapeDtypeStruct((rows, width), BF16),
            jax.ShapeDtypeStruct((pairs, 2 * rows, 1), F32),
        ],
        scratch_shapes=scratch,
        compiler_params=pltpu.CompilerParams(vmem_limit_bytes=VMEM_BYTES),
        cost_estimate=pl.CostEstimate(
            flops=16 * rows * width * seq, bytes_accessed=40_000_000, transcendentals=0
        ),
        name="attend_forward",
    )(queries, kv, qplace, kplace)


def attend_backward(queries, kv, qplace, kplace, attended, log_totals, grads):
    rows, width = queries.shape
    seq = kv.shape[0]
    pairs = width // (2 * DH)
    pair, lse, full, common, scratch = attention_specs(rows, seq)
    return pl.pallas_call(
        functools.partial(backward_kernel, pairs),
        grid=(pairs,),
        in_specs=common + [pair, lse, pair],
        out_specs=[pair, full((seq, 4 * DH))],
        out_shape=[
            jax.ShapeDtypeStruct((rows, width), BF16),
            jax.ShapeDtypeStruct((seq, 4 * DH), BF16),
        ],
        scratch_shapes=scratch + [pltpu.VMEM((2, 2, seq, 2 * DH), F32)],
        compiler_params=pltpu.CompilerParams(vmem_limit_bytes=VMEM_BYTES),
        cost_estimate=pl.CostEstimate(
            flops=40 * rows * width * seq, bytes_accessed=80_000_000, transcendentals=0
        ),
        name="attend_backward",
    )(queries, kv, qplace, kplace, attended, log_totals, grads)


def trade_rows(buffer):
    return lax.all_to_all(buffer, ("dp", "ctx"), split_axis=0, concat_axis=0, tiled=True)


def local(
    resid,
    queries,
    keys,
    values,
    block_order,
    routes,
    route_weights,
    norm_gain,
    w_gate,
    w_up,
    w_down,
    cotangent,
):
    tok_rows, model_width = resid.shape
    block_rows = tok_rows // 2
    ctx_count = lax.axis_size("ctx")
    seq_rows = tok_rows * ctx_count
    top_count = routes.shape[1]
    expert_count = lax.axis_size("dp") * ctx_count * w_gate.shape[0]
    capacity = max(2, 5 * tok_rows * top_count // (4 * expert_count))
    room = -(-capacity // 8) * 8
    slots_all = expert_count * room

    experts = jnp.arange(expert_count, dtype=jnp.int32)
    named = (routes[:, :, None] == experts[None, None, :]).astype(F32)
    token = jnp.arange(tok_rows, dtype=jnp.int32)
    earlier = (token[:, None] > token[None, :]).astype(BF16)
    before = dot_nn(earlier, jnp.sum(named, axis=1).astype(BF16))
    rank = jnp.sum(named * before[:, None, :], axis=2).astype(jnp.int32)
    flat_slots = routes * room + rank
    slot_ids = jnp.arange(slots_all, dtype=jnp.int32)
    slot_map = jnp.zeros((slots_all, tok_rows), F32)
    weight_map = jnp.zeros((slots_all, tok_rows), F32)
    for k in range(top_count):
        chosen = flat_slots[:, k][None, :] == slot_ids[:, None]
        slot_map = slot_map + chosen.astype(F32)
        weight_map = weight_map + jnp.where(chosen, route_weights[:, k][None, :], 0.0)
    dispatch = slot_map.astype(BF16)
    slot_weights = jnp.sum(weight_map, axis=1, keepdims=True)
    weight_high = weight_map.astype(BF16)
    weight_low = (weight_map - weight_high.astype(F32)).astype(BF16)
    buffer_shape = (expert_count, room, model_width)

    grad_send = (slot_weights * dot_nn(dispatch, cotangent)).astype(BF16).reshape(buffer_shape)
    kv = lax.all_gather(jnp.concatenate([keys, values], axis=1), "ctx", axis=0, tiled=True)
    grad_recv = trade_rows(grad_send).reshape(-1, model_width)

    within = jnp.arange(block_rows, dtype=jnp.int32)
    kplace = (block_order[:, None] * block_rows + within[None, :]).reshape(1, seq_rows)
    own_blocks = lax.dynamic_slice_in_dim(block_order, 2 * lax.axis_index("ctx"), 2, 0)
    qplace = (own_blocks[:, None] * block_rows + within[None, :]).reshape(tok_rows, 1)
    attended, log_totals = attend_forward(queries, kv, qplace, kplace)

    hidden = (resid.astype(F32) + attended.astype(F32)).astype(BF16)
    hidden_f = hidden.astype(F32)
    inv_rms = lax.rsqrt(jnp.mean(hidden_f * hidden_f, axis=-1, keepdims=True) + EPSILON)
    normed = (hidden_f * inv_rms * norm_gain).astype(BF16)
    send_rows = dot_nn(dispatch, normed).astype(BF16).reshape(buffer_shape)
    received = trade_rows(send_rows).reshape(-1, model_width)

    gate_w, up_w, down_w = w_gate[0], w_up[0], w_down[0]
    gate_lin = dot_nn(received, gate_w)
    up_lin = dot_nn(received, up_w)
    gate_sig = jax.nn.sigmoid(gate_lin)
    gate_act = gate_lin * gate_sig
    hidden_act = (gate_act * up_lin).astype(BF16)
    grad_act = dot_nt(grad_recv, down_w)
    grad_gate = (grad_act * up_lin * gate_sig * (1.0 + gate_lin * (1.0 - gate_sig))).astype(BF16)
    grad_up = (grad_act * gate_act).astype(BF16)
    grad_input = (dot_nt(grad_gate, gate_w) + dot_nt(grad_up, up_w)).astype(BF16)
    grad_back = trade_rows(grad_input.reshape(buffer_shape)).reshape(-1, model_width)
    produced = dot_nn(hidden_act, down_w).astype(BF16)
    produced, grad_back = lax.optimization_barrier((produced, grad_back))
    returned = trade_rows(produced.reshape(buffer_shape)).reshape(-1, model_width)
    d_w_gate = dot_tn(received, grad_gate).astype(BF16)[None]
    d_w_up = dot_tn(received, grad_up).astype(BF16)[None]
    d_w_down = dot_tn(hidden_act, grad_recv).astype(BF16)[None]

    grad_normed = dot_tn(dispatch, grad_back)
    grad_scaled = grad_normed * norm_gain
    grad_hidden = inv_rms * grad_scaled - hidden_f * inv_rms * inv_rms * inv_rms * jnp.mean(
        grad_scaled * hidden_f, axis=-1, keepdims=True
    )
    d_resid = (cotangent.astype(F32) + grad_hidden).astype(BF16)
    gain_terms = jnp.sum(grad_normed * hidden_f * inv_rms, axis=0)
    gains = lax.all_gather(gain_terms.reshape(-1, 128), ("dp", "ctx"), axis=0, tiled=False)
    d_gain = jnp.sum(gains, axis=0).reshape(-1)

    d_queries, d_kv = attend_backward(
        queries, kv, qplace, kplace, attended, log_totals, d_resid
    )
    kv_terms = lax.all_to_all(
        d_kv.reshape(ctx_count, tok_rows, -1), "ctx", split_axis=0, concat_axis=0, tiled=True
    )
    d_kv_mine = jnp.sum(kv_terms.astype(F32), axis=0).astype(BF16)

    mixed = dot_tn(weight_high, returned) + dot_tn(weight_low, returned)
    layer_out = (hidden_f + mixed).astype(BF16)
    width = keys.shape[1]
    return (
        layer_out,
        d_resid,
        d_queries,
        d_kv_mine[:, :width],
        d_kv_mine[:, width:],
        d_gain,
        d_w_gate,
        d_w_up,
        d_w_down,
    )


def solution(mesh):
    rows = P(("dp", "ctx"), None)
    stacks = P(("dp", "ctx"), None, None)
    return jax.shard_map(
        local,
        mesh=mesh,
        in_specs=(rows, rows, rows, rows, P(), rows, rows, P(), stacks, stacks, stacks, rows),
        out_specs=(rows, rows, rows, rows, rows, P(), stacks, stacks, stacks),
        check_vma=False,
    )
```

```python
import functools
import math

import jax
import jax.numpy as jnp
from jax import lax
from jax.experimental import pallas as pl
from jax.experimental.pallas import tpu as pltpu
from jax.sharding import PartitionSpec as P

DH = 64
NEG_BIG = -1e30
EPSILON = 1e-06
F32 = jnp.float32
BF16 = jnp.bfloat16
VMEM_BYTES = 48 * 1024 * 1024


def dot_nn(a, b):
    return lax.dot_general(a, b, (((1,), (0,)), ((), ())), preferred_element_type=F32)


def dot_nt(a, b):
    return lax.dot_general(a, b, (((1,), (1,)), ((), ())), preferred_element_type=F32)


def dot_tn(a, b):
    return lax.dot_general(a, b, (((0,), (0,)), ((), ())), preferred_element_type=F32)


def twin(block, head):
    lane = lax.broadcasted_iota(jnp.int32, block.shape, 1)
    turned = jnp.concatenate([block[:, DH:], block[:, :DH]], axis=1)
    return jnp.where((lane < DH) == (head == 0), block, turned)


def spread(block):
    lane = lax.broadcasted_iota(jnp.int32, block.shape, 1)
    zero = jnp.zeros_like(block)
    return jnp.concatenate(
        [jnp.where(lane < DH, block, zero), jnp.where(lane >= DH, block, zero)], axis=0
    )


def unspread(stacked):
    rows = stacked.shape[0] // 2
    lane = lax.broadcasted_iota(jnp.int32, (rows, stacked.shape[1]), 1)
    return jnp.where(lane < DH, stacked[:rows], stacked[rows:])


def prepare(kv_ref, qplace_ref, kplace_ref, bias, twins):
    width = kv_ref.shape[1] // 2
    bias[...] = jnp.where(qplace_ref[...] >= kplace_ref[...], 0.0, NEG_BIG).astype(F32)
    for part in range(2):
        block = kv_ref[:, part * width : (part + 1) * width].astype(F32)
        for head in range(2):
            twins[part, head] = twin(block, head).astype(BF16)


def masked_scores(q2, keys2, bias):
    scores = dot_nt(q2, keys2) * (DH**-0.5)
    rows = bias.shape[0]
    return jnp.concatenate([scores[:rows] + bias[...], scores[rows:] + bias[...]], axis=0)


def forward_kernel(pairs, q_ref, kv_ref, qplace_ref, kplace_ref, out_ref, lse_ref, bias, twins):
    step = pl.program_id(0)

    @pl.when(step == 0)
    def _():
        prepare(kv_ref, qplace_ref, kplace_ref, bias, twins)

    group = step // (pairs // 2)
    scores = masked_scores(spread(q_ref[...]), twins[0, group], bias)
    top = jnp.max(scores, axis=1, keepdims=True)
    weights = jnp.exp(scores - top)
    total = jnp.sum(weights, axis=1, keepdims=True)
    mixed = dot_nn(weights.astype(BF16), twins[1, group])
    out_ref[...] = unspread(mixed / total).astype(BF16)
    lse_ref[0] = top + jnp.log(total)


def backward_kernel(
    pairs,
    q_ref,
    kv_ref,
    qplace_ref,
    kplace_ref,
    att_ref,
    lse_ref,
    grad_ref,
    dq_ref,
    dkv_ref,
    bias,
    twins,
    sums,
):
    step = pl.program_id(0)

    @pl.when(step == 0)
    def _():
        prepare(kv_ref, qplace_ref, kplace_ref, bias, twins)
        sums[...] = jnp.zeros_like(sums)

    group = step // (pairs // 2)
    q2 = spread(q_ref[...])
    g2 = spread(grad_ref[...])
    keys2 = twins[0, group]
    probs = jnp.exp(masked_scores(q2, keys2, bias) - lse_ref[0])
    product = grad_ref[...].astype(F32) * att_ref[...].astype(F32)
    row_dots = jnp.sum(spread(product), axis=1, keepdims=True)
    grad_probs = dot_nt(g2, twins[1, group])
    grad_scores = (probs * (grad_probs - row_dots) * (DH**-0.5)).astype(BF16)
    dq_ref[...] = unspread(dot_nn(grad_scores, keys2)).astype(BF16)
    sums[0, group] += dot_tn(grad_scores, q2)
    sums[1, group] += dot_tn(probs.astype(BF16), g2)

    @pl.when(step == pairs - 1)
    def _():
        width = dkv_ref.shape[1] // 2
        for part in range(2):
            folded = []
            for head in range(2):
                both = sums[part, head]
                folded.append(
                    both + jnp.concatenate([both[:, DH:], both[:, :DH]], axis=1)
                )
            lane = lax.broadcasted_iota(jnp.int32, folded[0].shape, 1)
            dkv_ref[:, part * width : (part + 1) * width] = jnp.where(
                lane < DH, folded[0], folded[1]
            ).astype(BF16)


def attention_specs(rows, seq):
    pair = pl.BlockSpec((rows, 2 * DH), lambda i: (0, i))
    lse = pl.BlockSpec((1, 2 * rows, 1), lambda i: (i, 0, 0))
    full = lambda shape: pl.BlockSpec(shape, lambda i: (0, 0))
    common = [pair, full((seq, 4 * DH)), full((rows, 1)), full((1, seq))]
    scratch = [pltpu.VMEM((rows, seq), F32), pltpu.VMEM((2, 2, seq, 2 * DH), BF16)]
    return pair, lse, full, common, scratch


def attend_forward(queries, kv, qplace, kplace):
    rows, width = queries.shape
    seq = kv.shape[0]
    pairs = width // (2 * DH)
    pair, lse, full, common, scratch = attention_specs(rows, seq)
    return pl.pallas_call(
        functools.partial(forward_kernel, pairs),
        grid=(pairs,),
        in_specs=common,
        out_specs=[pair, lse],
        out_shape=[
            jax.ShapeDtypeStruct((rows, width), BF16),
            jax.ShapeDtypeStruct((pairs, 2 * rows, 1), F32),
        ],
        scratch_shapes=scratch,
        compiler_params=pltpu.CompilerParams(vmem_limit_bytes=VMEM_BYTES),
        cost_estimate=pl.CostEstimate(
            flops=16 * rows * width * seq, bytes_accessed=40_000_000, transcendentals=0
        ),
        name="attend_forward",
    )(queries, kv, qplace, kplace)


def attend_backward(queries, kv, qplace, kplace, attended, log_totals, grads):
    rows, width = queries.shape
    seq = kv.shape[0]
    pairs = width // (2 * DH)
    pair, lse, full, common, scratch = attention_specs(rows, seq)
    return pl.pallas_call(
        functools.partial(backward_kernel, pairs),
        grid=(pairs,),
        in_specs=common + [pair, lse, pair],
        out_specs=[pair, full((seq, 4 * DH))],
        out_shape=[
            jax.ShapeDtypeStruct((rows, width), BF16),
            jax.ShapeDtypeStruct((seq, 4 * DH), BF16),
        ],
        scratch_shapes=scratch + [pltpu.VMEM((2, 2, seq, 2 * DH), F32)],
        compiler_params=pltpu.CompilerParams(vmem_limit_bytes=VMEM_BYTES),
        cost_estimate=pl.CostEstimate(
            flops=40 * rows * width * seq, bytes_accessed=80_000_000, transcendentals=0
        ),
        name="attend_backward",
    )(queries, kv, qplace, kplace, attended, log_totals, grads)


def regroup_kernel(moves, chunks_in, chunks_out, move_ref, in_ref, out_ref):
    width_in = in_ref.shape[1] // chunks_in
    width_out = out_ref.shape[1] // chunks_out
    if chunks_in == 1:
        for h in range(moves):
            part = dot_nn(move_ref[h], in_ref[...])
            out_ref[:, h * width_out : (h + 1) * width_out] = part.astype(BF16)
    else:
        total = dot_nn(move_ref[0], in_ref[:, :width_in])
        for h in range(1, moves):
            total += dot_nn(move_ref[h], in_ref[:, h * width_in : (h + 1) * width_in])
        out_ref[...] = total.astype(BF16)


def regroup(array, moves, chunks_in, chunks_out, name):
    count, rows_out, rows_in = moves.shape
    steps = array.shape[0] // rows_in
    width_out = array.shape[1] // chunks_in * chunks_out
    return pl.pallas_call(
        functools.partial(regroup_kernel, count, chunks_in, chunks_out),
        grid=(steps,),
        in_specs=[
            pl.BlockSpec(moves.shape, lambda i: (0, 0, 0)),
            pl.BlockSpec((rows_in, array.shape[1]), lambda i: (i, 0)),
        ],
        out_specs=pl.BlockSpec((rows_out, width_out), lambda i: (i, 0)),
        out_shape=jax.ShapeDtypeStruct((steps * rows_out, width_out), BF16),
        compiler_params=pltpu.CompilerParams(vmem_limit_bytes=VMEM_BYTES),
        cost_estimate=pl.CostEstimate(
            flops=2 * array.size * rows_out, bytes_accessed=4 * array.size, transcendentals=0
        ),
        name=name,
    )(moves, array)


def trade_rows(buffer):
    return lax.all_to_all(buffer, ("dp", "ctx"), split_axis=0, concat_axis=0, tiled=True)


def local(
    resid,
    queries,
    keys,
    values,
    block_order,
    routes,
    route_weights,
    norm_gain,
    w_gate,
    w_up,
    w_down,
    cotangent,
):
    tok_rows, model_width = resid.shape
    block_rows = tok_rows // 2
    ctx_count = lax.axis_size("ctx")
    seq_rows = tok_rows * ctx_count
    top_count = routes.shape[1]
    expert_count = lax.axis_size("dp") * ctx_count * w_gate.shape[0]
    capacity = max(2, 5 * tok_rows * top_count // (4 * expert_count))
    room = -(-(capacity + 2) // 8) * 8
    slots_all = expert_count * room

    experts = jnp.arange(expert_count, dtype=jnp.int32)
    named = (routes[:, :, None] == experts[None, None, :]).astype(F32)
    token = jnp.arange(tok_rows, dtype=jnp.int32)
    earlier = (token[:, None] > token[None, :]).astype(BF16)
    before = dot_nn(earlier, jnp.sum(named, axis=1).astype(BF16))
    rank = jnp.sum(named * before[:, None, :], axis=2).astype(jnp.int32)
    folds = 8 // math.gcd(capacity, 8)
    fold_width = model_width // folds
    packed_rows = folds * capacity
    packed_shape = (expert_count, packed_rows, fold_width)

    def fold(block):
        return jnp.concatenate(
            [block[:, h * fold_width : (h + 1) * fold_width] for h in range(folds)], axis=0
        )

    def unfold(block):
        return jnp.concatenate(
            [block[h * tok_rows : (h + 1) * tok_rows] for h in range(folds)], axis=1
        )

    packed_ids = jnp.arange(expert_count * packed_rows, dtype=jnp.int32)
    packed_slot = packed_ids // packed_rows * capacity + packed_ids % capacity
    packed_key = packed_slot * folds + packed_ids // capacity % folds
    column_fold = jnp.arange(folds, dtype=jnp.int32)[:, None]
    slot_map = jnp.zeros((expert_count * packed_rows, folds * tok_rows), F32)
    slot_weights = jnp.zeros((expert_count * packed_rows, 1), F32)
    slot_ids = jnp.arange(slots_all, dtype=jnp.int32)
    weight_map = jnp.zeros((slots_all, tok_rows), F32)
    for k in range(top_count):
        taken = (routes[:, k] * capacity + rank[:, k])[None, :] * folds + column_fold
        chosen = taken.reshape(1, -1) == packed_key[:, None]
        slot_map = slot_map + chosen.astype(F32)
        weight = jnp.tile(route_weights[:, k], folds)[None, :]
        slot_weights = slot_weights + jnp.sum(
            jnp.where(chosen, weight, 0.0), axis=1, keepdims=True
        )
        returned_slot = (routes[:, k] * room + rank[:, k])[None, :]
        weight_map = weight_map + jnp.where(
            returned_slot == slot_ids[:, None], route_weights[:, k][None, :], 0.0
        )
    dispatch = slot_map.astype(BF16)
    weight_high = weight_map.astype(BF16)
    weight_low = (weight_map - weight_high.astype(F32)).astype(BF16)
    buffer_shape = (expert_count, room, model_width)

    batch = 16 // math.gcd(capacity, 16)
    row_at = jnp.arange(batch * capacity, dtype=jnp.int32)
    first_packed = row_at // capacity * packed_rows + row_at % capacity
    packed_at = jnp.arange(batch * packed_rows, dtype=jnp.int32)
    unpack_moves = jnp.stack(
        [first_packed[:, None] + h * capacity == packed_at[None, :] for h in range(folds)]
    ).astype(BF16)
    pack_moves = jnp.swapaxes(unpack_moves, 1, 2)
    room_at = jnp.arange(batch * room, dtype=jnp.int32)
    room_moves = (
        room_at[:, None] == (row_at // capacity * room + row_at % capacity)[None, :]
    ).astype(BF16)[None]

    kv = lax.all_gather(jnp.concatenate([keys, values], axis=1), "ctx", axis=0, tiled=True)
    grad_send = (slot_weights * dot_nn(dispatch, fold(cotangent))).astype(BF16)
    kv, grad_send = lax.optimization_barrier((kv, grad_send))
    grad_packed = trade_rows(grad_send.reshape(packed_shape)).reshape(-1, fold_width)

    within = jnp.arange(block_rows, dtype=jnp.int32)
    kplace = (block_order[:, None] * block_rows + within[None, :]).reshape(1, seq_rows)
    own_blocks = lax.dynamic_slice_in_dim(block_order, 2 * lax.axis_index("ctx"), 2, 0)
    qplace = (own_blocks[:, None] * block_rows + within[None, :]).reshape(tok_rows, 1)
    attended, log_totals = attend_forward(queries, kv, qplace, kplace)

    hidden = (resid.astype(F32) + attended.astype(F32)).astype(BF16)
    hidden_f = hidden.astype(F32)
    inv_rms = lax.rsqrt(jnp.mean(hidden_f * hidden_f, axis=-1, keepdims=True) + EPSILON)
    normed = (hidden_f * inv_rms * norm_gain).astype(BF16)
    send_rows = dot_nn(dispatch, fold(normed)).astype(BF16)
    send_rows, grad_packed = lax.optimization_barrier((send_rows, grad_packed))
    packed = trade_rows(send_rows.reshape(packed_shape)).reshape(-1, fold_width)
    grad_recv = regroup(grad_packed, unpack_moves, 1, folds, "unpack_grads")
    received = regroup(packed, unpack_moves, 1, folds, "unpack_rows")

    gate_w, up_w, down_w = w_gate[0], w_up[0], w_down[0]
    gate_lin = dot_nn(received, gate_w)
    up_lin = dot_nn(received, up_w)
    gate_sig = jax.nn.sigmoid(gate_lin)
    gate_act = gate_lin * gate_sig
    hidden_act = (gate_act * up_lin).astype(BF16)
    grad_act = dot_nt(grad_recv, down_w)
    grad_gate = (grad_act * up_lin * gate_sig * (1.0 + gate_lin * (1.0 - gate_sig))).astype(BF16)
    grad_up = (grad_act * gate_act).astype(BF16)
    grad_input = (dot_nt(grad_gate, gate_w) + dot_nt(grad_up, up_w)).astype(BF16)
    grad_input = regroup(grad_input, pack_moves, folds, 1, "pack_grads")
    grad_back = trade_rows(grad_input.reshape(packed_shape)).reshape(-1, fold_width)
    produced = regroup(dot_nn(hidden_act, down_w).astype(BF16), room_moves, 1, 1, "place_rows")
    d_w_gate = dot_tn(received, grad_gate).astype(BF16)
    d_w_up = dot_tn(received, grad_up).astype(BF16)
    d_w_down = dot_tn(hidden_act, grad_recv).astype(BF16)
    produced, grad_back, d_w_gate, d_w_up, d_w_down = lax.optimization_barrier(
        (produced, grad_back, d_w_gate, d_w_up, d_w_down)
    )

    grad_normed = unfold(dot_tn(dispatch, grad_back))
    grad_scaled = grad_normed * norm_gain
    grad_hidden = inv_rms * grad_scaled - hidden_f * inv_rms * inv_rms * inv_rms * jnp.mean(
        grad_scaled * hidden_f, axis=-1, keepdims=True
    )
    d_resid = (cotangent.astype(F32) + grad_hidden).astype(BF16)
    gain_terms = jnp.sum(grad_normed * hidden_f * inv_rms, axis=0)
    gain_high = gain_terms.astype(BF16)
    gain_low = (gain_terms - gain_high.astype(F32)).astype(BF16)
    gain_rows = jnp.broadcast_to(
        jnp.stack([gain_high, gain_low])[None], (expert_count, 2, model_width)
    )
    outgoing = lax.dynamic_update_slice(
        produced.reshape(buffer_shape), gain_rows, (0, capacity, 0)
    )
    outgoing, d_resid = lax.optimization_barrier((outgoing, d_resid))
    returned = trade_rows(outgoing).reshape(-1, model_width)

    d_queries, d_kv = attend_backward(
        queries, kv, qplace, kplace, attended, log_totals, d_resid
    )
    d_kv, returned = lax.optimization_barrier((d_kv, returned))
    kv_terms = lax.all_to_all(
        d_kv.reshape(ctx_count, tok_rows, -1), "ctx", split_axis=0, concat_axis=0, tiled=True
    )
    d_kv_mine = jnp.sum(kv_terms.astype(F32), axis=0).astype(BF16)

    place = slot_ids % room
    gain_slots = ((place >= capacity) & (place < capacity + 2)).astype(BF16)
    gain_columns = jnp.broadcast_to(gain_slots[:, None], (slots_all, 128))
    readers = jnp.concatenate([weight_high, weight_low, gain_columns], axis=1)
    combined = dot_tn(readers, returned)
    layer_out = (hidden_f + combined[:tok_rows] + combined[tok_rows : 2 * tok_rows]).astype(BF16)
    d_gain = combined[2 * tok_rows]
    width = keys.shape[1]
    return (
        layer_out,
        d_resid,
        d_queries,
        d_kv_mine[:, :width],
        d_kv_mine[:, width:],
        d_gain,
        d_w_gate[None],
        d_w_up[None],
        d_w_down[None],
    )


def solution(mesh):
    rows = P(("dp", "ctx"), None)
    stacks = P(("dp", "ctx"), None, None)
    return jax.shard_map(
        local,
        mesh=mesh,
        in_specs=(rows, rows, rows, rows, P(), rows, rows, P(), stacks, stacks, stacks, rows),
        out_specs=(rows, rows, rows, rows, rows, P(), stacks, stacks, stacks),
        check_vma=False,
    )
```
